32 devices in a mesh: term: 2 (over y), blk: 16 (over z, x, core).
Axes of the slice: x: 2, y: 2, z: 4, core: 2. Of those that a mesh axis runs over, the one named last changes fastest.
Arguments:
- start_vec: float32 [4, 32, 128, 128], P(None, 'blk', 'term'), may hold values from -6 to 6
- left_env: float32 [8, 32, 128, 128], P('term', 'blk'), may hold values from -0.5 to 0.5
- right_env: float32 [8, 32, 128, 128], P('term', 'blk'), may hold values from -0.5 to 0.5
- local_mpo: float32 [8, 4, 4], P('term'), may hold values from -1 to 1
- term_charge: int32 [8], P('term'), may hold values from -1 to 1, as said below
- sector_sizes: int32 [32], P('blk'), may hold values from 64 to 128, as said below
- sector_ranks: int32 [32], P('blk'), may hold values from 32 to 128, as said below
Outputs:
- coeffs: float32 [2, 8], replicated
- krylov: float32 [4, 32, 128, 128], P(None, 'blk', 'term')
- density: float32 [32, 128, 128], P('blk', 'term')
The draws below stay inside these ranges and needn't reach their ends.
Inputs may be any that keep to these rules, and one draw needn't show every extreme that they name: `term_charge`: each term moves charge by -1, 0 or +1; some term moves +1 and some -1 in every draw, and some moves 0 when 8 is 3 or more. `sector_sizes`: some sector is full in every draw. `sector_ranks`: no sector keeps more states than it has live, and some sector keeps all 128.
All inputs are finite; a program needn't handle non-finite values.
Results may differ from the reference program's by a relative error of at most 0.0003.
Values sent between devices are 32-bit elements; how exact they have to be, the bound alone decides.
A program may use at most 64 MiB of HBM per device.

```python
import jax
import jax.numpy as jnp
from jax import lax

NSEC = 32
BS = 128
P_SIZE = 4
W = 8
KRY = 8


def sector_pair(key):
    first = jax.random.fold_in(key, 301)
    second = jax.random.fold_in(key, 302)
    third = jax.random.fold_in(key, 303)
    sizes = jax.random.randint(first, (NSEC,), BS // 2, BS + 1).astype(jnp.int32)
    chosen = jax.random.randint(second, (), 0, NSEC).astype(jnp.int32)
    sizes = sizes.at[chosen].set(BS)
    cuts = jax.random.randint(third, (NSEC,), 0, BS // 4 + 1).astype(jnp.int32)
    ranks = sizes - cuts
    ranks = ranks.at[chosen].set(BS)
    return (sizes, ranks)


def draw_sector_sizes(key, part):
    return sector_pair(key)[0]


def draw_sector_ranks(key, part):
    return sector_pair(key)[1]


def draw_term_charge(key, part):
    pattern = (jnp.arange(W, dtype=jnp.int32) + 2) % 3 - 1
    order = jax.random.permutation(jax.random.fold_in(key, 411), W).astype(jnp.int32)
    return pattern[order].astype(jnp.int32)


def levels(own_key, extent, shards, low, high):
    factor_of = 1.0
    for position, blocks in shards:
        draws = jax.random.uniform(jax.random.fold_in(jax.random.fold_in(own_key, 6), position), (blocks,), jnp.float32, low / len(shards), high / len(shards))
        factor_of = factor_of * jnp.repeat(jnp.exp(draws), extent[position] // blocks).reshape((-1,) + (1,) * (len(extent) - 1 - position))
    return factor_of


def normal_values(own_key, extent, scale, reach, cuts=(), held_as=jnp.bfloat16):
    array = scale * jax.random.normal(own_key, extent, jnp.float32)
    if cuts:
        array = array * levels(own_key, extent, cuts, -0.22, 0.18)
    return jnp.clip(array, -reach, reach).astype(held_as)


def setup_inputs(seed: int = 0) -> dict:
    streams_of = jax.random.split(jax.random.key(seed), 8)
    return {
        "start_vec": normal_values(streams_of[0], (P_SIZE, NSEC, BS, BS), 1.0, 6.0, ((1, 16), (2, 2)), jnp.float32),
        "left_env": normal_values(streams_of[1], (W, NSEC, BS, BS), BS ** -0.5, 0.5, ((0, 2), (1, 16)), jnp.float32),
        "right_env": normal_values(streams_of[2], (W, NSEC, BS, BS), BS ** -0.5, 0.5, ((0, 2), (1, 16)), jnp.float32),
        "local_mpo": normal_values(streams_of[3], (W, P_SIZE, P_SIZE), (W * P_SIZE) ** -0.5, 1.0, ((0, 2),), jnp.float32),
        "term_charge": draw_term_charge(jax.random.fold_in(streams_of[7], 71), 0),
        "sector_sizes": draw_sector_sizes(jax.random.fold_in(streams_of[7], 71), 0),
        "sector_ranks": draw_sector_ranks(jax.random.fold_in(streams_of[7], 71), 0),
    }


HI = lax.Precision.HIGHEST

def live_mask(counts, width):
    return (jnp.arange(width, dtype=jnp.int32)[None, :] < counts[:, None]).astype(jnp.float32)

def shifted_sectors(vector, upward):
    zero_block = jnp.zeros_like(vector[:, :1])
    if upward:
        return jnp.concatenate([zero_block, vector[:, :-1]], axis=1)
    return jnp.concatenate([vector[:, 1:], zero_block], axis=1)

def apply_operator(vector, left_env, right_env, local_mpo, term_charge, mask):
    below = shifted_sectors(vector, True)
    above = shifted_sectors(vector, False)

    def one_term(total, pieces):
        left, right, mixer, charge = pieces
        source = jnp.where(charge == 1, below, jnp.where(charge == -1, above, vector))
        mixed = jnp.einsum('pq,qiab->piab', mixer, source, precision=HI)
        inner = jnp.einsum('iac,picb->piab', left, mixed, precision=HI)
        outer = jnp.einsum('piac,ibc->piab', inner, right, precision=HI)
        return (total + outer, None)
    total, _ = lax.scan(one_term, jnp.zeros_like(vector), (left_env, right_env, local_mpo, term_charge))
    return total * mask

def reference(start_vec, left_env, right_env, local_mpo, term_charge, sector_sizes, sector_ranks):
    width = start_vec.shape[2]
    sectors = start_vec.shape[1]
    states = start_vec.shape[0]
    live = live_mask(sector_sizes, width)
    mask = (live[:, :, None] * live[:, None, :])[None]
    start = start_vec * mask
    vector = start / jnp.sqrt(jnp.sum(start * start) + 1e-06)
    previous = jnp.zeros_like(vector)
    beta = jnp.float32(0.0)
    alphas = []
    betas = []
    for step in range(KRY):
        image = apply_operator(vector, left_env, right_env, local_mpo, term_charge, mask)
        alpha = jnp.sum(vector * image)
        resid = image - alpha * vector - beta * previous
        new_beta = jnp.sqrt(jnp.sum(resid * resid) + 1e-06)
        previous = vector
        vector = resid / new_beta
        beta = new_beta
        alphas.append(alpha)
        betas.append(new_beta)
    coeffs = jnp.stack([jnp.stack(alphas), jnp.stack(betas)]).astype(jnp.float32)
    krylov = jnp.sqrt(jnp.float32(sectors * states)) * width * vector
    kept = live_mask(sector_ranks, width)
    gram = jnp.einsum('piab,picb->iac', vector, vector, precision=HI)
    density = sectors * width * gram * kept[:, :, None] * kept[:, None, :]
    return (coeffs, krylov, density)
```

```python
import jax
import jax.numpy as jnp
from jax import lax
from jax.sharding import PartitionSpec as P
from jax.experimental import pallas as pl
from jax.experimental.pallas import tpu as pltpu

KRY = 8


HI = lax.Precision.HIGHEST


def from_behind(value, axis, by):
    devices = lax.axis_size(axis)
    pairs = [(i, i + by) for i in range(devices) if 0 <= i + by < devices]
    return lax.ppermute(value, axis, pairs)


def live_mask(counts, width):
    return (jnp.arange(width, dtype=jnp.int32)[None, :] < counts[:, None]).astype(jnp.float32)


def apply_operator(rows_vec, left_env, right_env, local_mpo, term_charge, row_mask):
    whole = lax.all_gather(rows_vec, "term", axis=2, tiled=True)
    lower_edge = from_behind(whole[:, -1:], "blk", 1)
    upper_edge = from_behind(whole[:, :1], "blk", -1)
    below = jnp.concatenate([lower_edge, whole[:, :-1]], axis=1)
    above = jnp.concatenate([whole[:, 1:], upper_edge], axis=1)
    partial_value = jnp.zeros_like(whole)
    for term_idx in range(left_env.shape[0]):
        charge = term_charge[term_idx]
        source = jnp.where(charge == 1, below, jnp.where(charge == -1, above, whole))
        mixed = jnp.einsum("pq,qiab->piab", local_mpo[term_idx], source, precision=HI)
        inner = jnp.einsum("iac,picb->piab", left_env[term_idx], mixed, precision=HI)
        partial_value = partial_value + jnp.einsum(
            "piac,ibc->piab", inner, right_env[term_idx], precision=HI
        )
    summed = lax.psum_scatter(partial_value, "term", scatter_dimension=2, tiled=True)
    return summed * row_mask


def per_device(start_vec, left_env, right_env, local_mpo, term_charge, sector_sizes, sector_ranks):
    width = start_vec.shape[3]
    row_count = start_vec.shape[2]
    states = start_vec.shape[0]
    sectors = start_vec.shape[1] * lax.axis_size("blk")
    row_start = lax.axis_index("term") * row_count
    row_ids = row_start + jnp.arange(row_count, dtype=jnp.int32)
    col_live = live_mask(sector_sizes, width)
    row_live = (row_ids[None, :] < sector_sizes[:, None]).astype(jnp.float32)
    row_mask = (row_live[:, :, None] * col_live[:, None, :])[None]
    start = start_vec * row_mask
    start_sq = lax.psum(jnp.sum(start * start), ("term", "blk"))
    vector = start / jnp.sqrt(start_sq + 1e-06)
    previous = jnp.zeros_like(vector)
    beta = jnp.float32(0.0)
    alphas = []
    betas = []
    for step in range(KRY):
        image = apply_operator(vector, left_env, right_env, local_mpo, term_charge, row_mask)
        alpha = lax.psum(jnp.sum(vector * image), ("term", "blk"))
        resid = image - alpha * vector - beta * previous
        norm_sq = lax.psum(jnp.sum(resid * resid), ("term", "blk"))
        new_beta = jnp.sqrt(norm_sq + 1e-06)
        previous = vector
        vector = resid / new_beta
        beta = new_beta
        alphas.append(alpha)
        betas.append(new_beta)
    coeffs = jnp.stack([jnp.stack(alphas), jnp.stack(betas)])
    krylov = jnp.sqrt(jnp.float32(sectors * states)) * width * vector
    whole = lax.all_gather(vector, "term", axis=2, tiled=True)
    gram = jnp.einsum("piab,picb->iac", vector, whole, precision=HI)
    kept_rows = (row_ids[None, :] < sector_ranks[:, None]).astype(jnp.float32)
    kept_cols = live_mask(sector_ranks, width)
    density = sectors * width * gram * kept_rows[:, :, None] * kept_cols[:, None, :]
    return (coeffs, krylov, density)


MESH = pl.DeviceIdType.MESH
BF = jnp.bfloat16
F32 = jnp.float32


def split(value):
    high = value.astype(BF)
    low = (value - high.astype(F32)).astype(BF)
    return high, low


def mm(left, right):
    return jnp.dot(left, right, preferred_element_type=F32)


def mm_t(left, right):
    return lax.dot_general(left, right, (((1,), (1,)), ((), ())), preferred_element_type=F32)


def lanczos_kernel(
    groups,
    start_ref, left_ref, right_ref, meta_ref, sizes_ref, ranks_ref,
    coeffs_ref, krylov_ref, density_ref,
    x_send, l_send, r_send, x_got, l_got, r_got, meta_got,
    images, vectors, below, above,
    l_split, r_split, mixed, applied,
    pair_sums, all_sums, marks, out_send, den_send, den_got,
    init_send, init_recv, meta_send, meta_recv,
    halo_send, halo_recv, pair_send, pair_recv, all_send, all_recv,
    out_ssem, out_rsem,
):
    states, _, rows, width = start_ref.shape
    terms = left_ref.shape[0]
    t = lax.axis_index("term")
    b = lax.axis_index("blk")
    k = b // 2
    c = b % 2
    flip = k % 2
    me = t * 2 + c
    half = (t + flip) % 2
    part = (c + half) % 2
    sector = 4 * k + 2 * half + part
    has_lower = sector > 0
    has_upper = sector < 4 * groups - 1

    def owner(index):
        group = index // 4
        rest = index % 4
        own_half = rest // 2
        own_part = rest % 2
        return ((own_half + group) % 2, group * 2 + (own_part + own_half) % 2)

    lower_dev = owner(jnp.maximum(sector - 1, 0))
    upper_dev = owner(jnp.minimum(sector + 1, 4 * groups - 1))

    def pair_dev(step):
        other = (me + step) % 4
        return other, (other // 2, k * 2 + other % 2)

    def group_dev(step):
        other = (k + step) % groups
        return other, (t, other * 2 + c)

    below[...] = jnp.zeros_like(below)
    above[...] = jnp.zeros_like(above)
    images[...] = jnp.zeros_like(images)
    vectors[...] = jnp.zeros_like(vectors)

    barrier = pltpu.get_barrier_semaphore()
    for step in range(1, 4):
        pl.semaphore_signal(barrier, inc=1, device_id=pair_dev(step)[1], device_id_type=MESH)
    for step in range(1, groups):
        pl.semaphore_signal(barrier, inc=1, device_id=group_dev(step)[1], device_id_type=MESH)

    row_ids = lax.broadcasted_iota(jnp.int32, (width, width), 0)
    col_ids = lax.broadcasted_iota(jnp.int32, (rows, width), 1)
    sub_ids = lax.broadcasted_iota(jnp.int32, (rows, width), 0) + t * rows
    for s in range(2):
        size = sizes_ref[s]
        live = (sub_ids < size) & (col_ids < size)
        for p in range(states):
            x_send[s, p] = jnp.where(live, start_ref[p, s], 0.0)
        for w in range(terms):
            l_send[s, w] = jnp.where(row_ids < size, left_ref[w, s], 0.0)
            r_send[s, w] = jnp.where(row_ids < size, right_ref[w, s], 0.0)

    pl.semaphore_wait(barrier, 3 + groups - 1)

    pieces = ((x_send, x_got), (l_send, l_got), (r_send, r_got))
    target_t = (c + flip) % 2

    def init_copy(s, j):
        src, dst = pieces[j]
        return pltpu.make_async_remote_copy(
            src_ref=src.at[s], dst_ref=dst.at[t],
            send_sem=init_send.at[s, j], recv_sem=init_recv.at[t, j],
            device_id=(target_t, k * 2 + (s + c) % 2), device_id_type=MESH,
        )

    keeps = target_t == t
    partner = pair_dev(2)[1]
    meta_copy = pltpu.make_async_remote_copy(
        src_ref=meta_ref, dst_ref=meta_got.at[t],
        send_sem=meta_send, recv_sem=meta_recv,
        device_id=partner, device_id_type=MESH,
    )
    for j in range(3):
        @pl.when(jnp.logical_not(keeps))
        def _():
            init_copy(0, j).start()
        init_copy(1, j).start()
        if j == 0:
            meta_copy.start()

    @pl.when(keeps)
    def _():
        x_got[t] = x_send[0]
        l_got[t] = l_send[0]
        r_got[t] = r_send[0]

    meta_got[t] = meta_ref[...]

    def init_wait(source, j):
        src, dst = pieces[j]
        @pl.when(jnp.logical_not((source == t) & (half == c)))
        def _():
            pltpu.make_async_remote_copy(
                src_ref=src.at[0], dst_ref=dst.at[source],
                send_sem=init_send.at[0, j], recv_sem=init_recv.at[source, j],
                device_id=partner, device_id_type=MESH,
            ).wait_recv()

    for source in range(2):
        init_wait(source, 0)
        images[0, :, pl.ds(source * rows, rows), :] = x_got[source]

    def lane_sums(first, second):
        total = first[0] * second[0]
        for p in range(1, states):
            total = total + first[p] * second[p]
        return jnp.sum(total, axis=0, keepdims=True)

    def write_products(slot, image, vector, before):
        pair_sums[slot, me] = jnp.concatenate(
            [
                lane_sums(image, image), lane_sums(vector, image), lane_sums(before, image),
                lane_sums(vector, vector), lane_sums(before, vector), lane_sums(before, before),
                jnp.zeros((2, width), F32),
            ],
            axis=0,
        )

    def pair_copy(slot, step):
        return pltpu.make_async_remote_copy(
            src_ref=pair_sums.at[slot, me], dst_ref=pair_sums.at[slot, me],
            send_sem=pair_send.at[step - 1], recv_sem=pair_recv.at[slot, me],
            device_id=pair_dev(step)[1], device_id_type=MESH,
        )

    def group_copy(slot, step):
        return pltpu.make_async_remote_copy(
            src_ref=all_sums.at[slot, k], dst_ref=all_sums.at[slot, k],
            send_sem=all_send.at[step - 1], recv_sem=all_recv.at[slot, k],
            device_id=group_dev(step)[1], device_id_type=MESH,
        )

    def start_pair(slot):
        for step in range(1, 4):
            pair_copy(slot, step).start()

    def finish_pair(slot):
        for step in range(1, 4):
            other, dev = pair_dev(step)
            pltpu.make_async_remote_copy(
                src_ref=pair_sums.at[slot, me], dst_ref=pair_sums.at[slot, other],
                send_sem=pair_send.at[step - 1], recv_sem=pair_recv.at[slot, other],
                device_id=dev, device_id_type=MESH,
            ).wait_recv()
        total = pair_sums[slot, 0]
        for other in range(1, 4):
            total = total + pair_sums[slot, other]
        all_sums[slot, k] = total
        for step in range(1, groups):
            group_copy(slot, step).start()

    def finish_sums(slot, beta_before):
        for step in range(1, groups):
            other, dev = group_dev(step)
            pltpu.make_async_remote_copy(
                src_ref=all_sums.at[slot, k], dst_ref=all_sums.at[slot, other],
                send_sem=all_send.at[step - 1], recv_sem=all_recv.at[slot, other],
                device_id=dev, device_id_type=MESH,
            ).wait_recv()
        total = all_sums[slot, 0]
        for other in range(1, groups):
            total = total + all_sums[slot, other]
        dots = jnp.sum(total, axis=1, keepdims=True)
        ww, vw, uw, vv, uv, uu = (dots[i:i + 1] for i in range(6))
        alpha = vw
        norm_sq = (
            ww - 2.0 * alpha * vw - 2.0 * beta_before * uw
            + alpha * alpha * vv + beta_before * beta_before * uu
            + 2.0 * alpha * beta_before * uv
        )
        beta = jnp.sqrt(jnp.maximum(norm_sq, 0.0) + 1e-06)
        for step in range(1, 4):
            pair_copy(slot, step).wait_send()
        for step in range(1, groups):
            group_copy(slot, step).wait_send()
        return alpha, beta

    def down_copy(slot):
        return pltpu.make_async_remote_copy(
            src_ref=images.at[slot], dst_ref=above.at[slot],
            send_sem=halo_send.at[0], recv_sem=halo_recv.at[slot, 0],
            device_id=lower_dev, device_id_type=MESH,
        )

    def up_copy(slot):
        return pltpu.make_async_remote_copy(
            src_ref=images.at[slot], dst_ref=below.at[slot],
            send_sem=halo_send.at[1], recv_sem=halo_recv.at[slot, 1],
            device_id=upper_dev, device_id_type=MESH,
        )

    def start_halo(slot):
        @pl.when(has_lower)
        def _():
            down_copy(slot).start()

        @pl.when(has_upper)
        def _():
            up_copy(slot).start()

    def wait_halo(slot):
        @pl.when(has_lower)
        def _():
            up_copy(slot).wait_recv()

        @pl.when(has_upper)
        def _():
            down_copy(slot).wait_recv()

    def wait_halo_send(slot):
        @pl.when(has_lower)
        def _():
            down_copy(slot).wait_send()

        @pl.when(has_upper)
        def _():
            up_copy(slot).wait_send()

    start_halo(0)
    first = images[0]
    write_products(0, first, vectors[0], vectors[1])
    start_pair(0)

    meta_copy.wait_recv()
    for source in range(2):
        init_wait(source, 1)
        for w in range(terms):
            high, low = split(l_got[source, w])
            l_split[source * terms + w] = jnp.concatenate([high, low], axis=1)
    for source in range(2):
        init_wait(source, 2)
        for w in range(terms):
            high, low = split(r_got[source, w].T)
            r_split[pl.ds((source * terms + w) * width, width), :] = jnp.concatenate([high, low], axis=1)

    def apply(slot):
        for w in range(2 * terms):
            source, local = w // terms, w % terms
            charge = meta_got[source, pl.ds(states * states * terms + local, 1), :]
            from_below = charge > 0.5
            from_above = charge < -0.5
            vec = jnp.concatenate(
                [
                    jnp.where(from_below, below[slot, q], jnp.where(from_above, above[slot, q], images[slot, q]))
                    for q in range(states)
                ],
                axis=1,
            )
            high, low = split(vec)
            both = l_split[w]
            inner = mm(both, jnp.concatenate([high, high], axis=0)) + mm(both[:, :width], low)
            for p in range(states):
                total = None
                for q in range(states):
                    row = local * states * states + p * states + q
                    factor = meta_got[source, pl.ds(row, 1), :]
                    piece = factor * inner[:, q * width:(q + 1) * width]
                    total = piece if total is None else total + piece
                high, low = split(total)
                mixed[pl.ds(p * width, width), pl.ds(w * width, width)] = high
                mixed[pl.ds((states + p) * width, width), pl.ds(w * width, width)] = low
        stacked = states * width
        top = mm(mixed[pl.ds(0, stacked), :], r_split[...])
        bottom = mm(mixed[pl.ds(stacked, stacked), :], r_split[:, :width])
        applied[...] = top[:, :width] + top[:, width:] + bottom

    lanes = lax.broadcasted_iota(jnp.int32, marks.shape, 1)
    subs = lax.broadcasted_iota(jnp.int32, marks.shape, 0)
    marks[...] = jnp.zeros_like(marks)

    def record(index, alpha, beta):
        here = lanes == index
        marks[...] = jnp.where(here & (subs == 0), alpha, jnp.where(here & (subs == 1), beta, marks[...]))

    def step_body(it, beta_before):
        slot = it % 2
        other = 1 - slot
        wait_halo(slot)
        finish_pair(slot)
        apply(slot)
        alpha, beta = finish_sums(slot, beta_before)
        record(it - 1, alpha, beta)
        scale = 1.0 / beta
        for p in range(states):
            image = images[slot, p]
            vector = vectors[slot, p]
            done = applied[pl.ds(p * width, width), :]
            vectors[other, p] = (image - alpha * vector - beta_before * vectors[other, p]) * scale
            images[other, p] = (done - alpha * image - beta_before * images[other, p]) * scale
        wait_halo_send(slot)

        @pl.when(it < KRY - 1)
        def _():
            start_halo(other)

        write_products(other, images[other], vectors[other], vectors[slot])
        start_pair(other)
        return jnp.where(it == 0, 0.0, beta)

    beta_before = lax.fori_loop(0, KRY, step_body, jnp.zeros((1, 1), F32))
    slot = KRY % 2
    finish_pair(slot)
    alpha, beta = finish_sums(slot, beta_before)
    record(KRY - 1, alpha, beta)
    coeffs_ref[...] = marks[:2, :KRY]
    scale = 1.0 / beta
    last = [
        (images[slot, p] - alpha * vectors[slot, p] - beta_before * vectors[1 - slot, p]) * scale
        for p in range(states)
    ]
    sectors = 4 * groups
    stretch = float((sectors * states) ** 0.5) * width
    for p in range(states):
        for r in range(2):
            out_send[r, p] = stretch * last[p][r * rows:(r + 1) * rows]

    def krylov_copy(r):
        return pltpu.make_async_remote_copy(
            src_ref=out_send.at[r], dst_ref=krylov_ref.at[:, part],
            send_sem=out_ssem.at[0, r], recv_sem=out_rsem.at[0, part],
            device_id=(r, k * 2 + half), device_id_type=MESH,
        )

    def density_copy(r):
        return pltpu.make_async_remote_copy(
            src_ref=den_send.at[r], dst_ref=den_got.at[part],
            send_sem=out_ssem.at[1, r], recv_sem=out_rsem.at[1, part],
            device_id=(r, k * 2 + half), device_id_type=MESH,
        )

    def is_self(r):
        return (t == r) & (half == c)

    for r in range(2):
        @pl.when(jnp.logical_not(is_self(r)))
        def _():
            krylov_copy(r).start()

        @pl.when(is_self(r))
        def _():
            for p in range(states):
                krylov_ref[p, part] = out_send[r, p]

    high, low = split(jnp.concatenate(last, axis=1))
    gram = mm_t(high, high) + mm_t(high, low) + mm_t(low, high)
    for r in range(2):
        den_send[r] = float(sectors * width) * gram[r * rows:(r + 1) * rows]
    for r in range(2):
        @pl.when(jnp.logical_not(is_self(r)))
        def _():
            density_copy(r).start()

        @pl.when(is_self(r))
        def _():
            den_got[part] = den_send[r]

    for s in range(2):
        @pl.when(jnp.logical_not(keeps & (s == 0)))
        def _():
            for which, src, dst in ((0, out_send.at[0], krylov_ref.at[:, s]), (1, den_send.at[0], den_got.at[s])):
                pltpu.make_async_remote_copy(
                    src_ref=src, dst_ref=dst,
                    send_sem=out_ssem.at[which, 0], recv_sem=out_rsem.at[which, s],
                    device_id=partner, device_id_type=MESH,
                ).wait_recv()
        rank = ranks_ref[s]
        kept = (sub_ids < rank) & (col_ids < rank)
        density_ref[s] = jnp.where(kept, den_got[s], 0.0)

    for r in range(2):
        @pl.when(jnp.logical_not(is_self(r)))
        def _():
            krylov_copy(r).wait_send()
            density_copy(r).wait_send()
    for j in range(3):
        @pl.when(jnp.logical_not(keeps))
        def _():
            init_copy(0, j).wait_send()
        init_copy(1, j).wait_send()
    meta_copy.wait_send()


def per_device_by_sector(start_vec, left_env, right_env, local_mpo, term_charge, sector_sizes, sector_ranks):
    states, _, rows, width = start_vec.shape
    terms = left_env.shape[0]
    groups = lax.axis_size("blk") // 2
    factors = jnp.concatenate([local_mpo.reshape(-1), term_charge.astype(F32)])
    pad = -factors.shape[0] % 8
    factors = jnp.pad(factors, (0, pad))
    meta = jnp.broadcast_to(factors[:, None], (factors.shape[0], width))
    block = (states, width, width)
    dma = pltpu.SemaphoreType.DMA
    vmem = pl.BlockSpec(memory_space=pltpu.VMEM)
    smem = pl.BlockSpec(memory_space=pltpu.SMEM)

    def kernel(*refs):
        lanczos_kernel(groups, *refs)

    return pl.pallas_call(
        kernel,
        out_shape=(
            jax.ShapeDtypeStruct((2, KRY), F32),
            jax.ShapeDtypeStruct(start_vec.shape, F32),
            jax.ShapeDtypeStruct((2, rows, width), F32),
        ),
        in_specs=[vmem, vmem, vmem, vmem, smem, smem],
        out_specs=(vmem, vmem, vmem),
        scratch_shapes=[
            pltpu.VMEM((2, states, rows, width), F32),
            pltpu.VMEM((2, terms, width, width), F32),
            pltpu.VMEM((2, terms, width, width), F32),
            pltpu.VMEM((2, states, rows, width), F32),
            pltpu.VMEM((2, terms, width, width), F32),
            pltpu.VMEM((2, terms, width, width), F32),
            pltpu.VMEM((2,) + meta.shape, F32),
            pltpu.VMEM((2,) + block, F32),
            pltpu.VMEM((2,) + block, F32),
            pltpu.VMEM((2,) + block, F32),
            pltpu.VMEM((2,) + block, F32),
            pltpu.VMEM((2 * terms, width, 2 * width), BF),
            pltpu.VMEM((2 * terms * width, 2 * width), BF),
            pltpu.VMEM((2 * states * width, 2 * terms * width), BF),
            pltpu.VMEM((states * width, width), F32),
            pltpu.VMEM((2, 4, 8, width), F32),
            pltpu.VMEM((2, groups, 8, width), F32),
            pltpu.VMEM((8, width), F32),
            pltpu.VMEM((2, states, rows, width), F32),
            pltpu.VMEM((2, rows, width), F32),
            pltpu.VMEM((2, rows, width), F32),
            dma((2, 3)), dma((2, 3)), dma, dma,
            dma((2,)), dma((2, 2)), dma((3,)), dma((2, 4)), dma((groups - 1,)), dma((2, groups)),
            dma((2, 2)), dma((2, 2)),
        ],
        compiler_params=pltpu.CompilerParams(
            collective_id=0, has_side_effects=True, vmem_limit_bytes=40 * 1024 * 1024
        ),
    )(start_vec, left_env, right_env, meta, sector_sizes, sector_ranks)


def solution(mesh):
    by_sector = mesh.shape["term"] == 2 and mesh.shape["blk"] % 2 == 0
    placed = (
        P(None, "blk", "term", None),
        P("term", "blk", None, None),
        P("term", "blk", None, None),
        P("term", None, None),
        P("term"),
        P("blk"),
        P("blk"),
    )
    return jax.shard_map(
        per_device_by_sector if by_sector else per_device,
        mesh=mesh,
        in_specs=placed,
        out_specs=(P(), P(None, "blk", "term", None), P("blk", "term", None)),
        check_vma=False,
    )
```

```python
import jax
import jax.numpy as jnp
from jax import lax
from jax.sharding import PartitionSpec as P
from jax.experimental import pallas as pl
from jax.experimental.pallas import tpu as pltpu

KRY = 8


HI = lax.Precision.HIGHEST


def from_behind(value, axis, by):
    devices = lax.axis_size(axis)
    pairs = [(i, i + by) for i in range(devices) if 0 <= i + by < devices]
    return lax.ppermute(value, axis, pairs)


def live_mask(counts, width):
    return (jnp.arange(width, dtype=jnp.int32)[None, :] < counts[:, None]).astype(jnp.float32)


def apply_operator(rows_vec, left_env, right_env, local_mpo, term_charge, row_mask):
    whole = lax.all_gather(rows_vec, "term", axis=2, tiled=True)
    lower_edge = from_behind(whole[:, -1:], "blk", 1)
    upper_edge = from_behind(whole[:, :1], "blk", -1)
    below = jnp.concatenate([lower_edge, whole[:, :-1]], axis=1)
    above = jnp.concatenate([whole[:, 1:], upper_edge], axis=1)
    partial_value = jnp.zeros_like(whole)
    for term_idx in range(left_env.shape[0]):
        charge = term_charge[term_idx]
        source = jnp.where(charge == 1, below, jnp.where(charge == -1, above, whole))
        mixed = jnp.einsum("pq,qiab->piab", local_mpo[term_idx], source, precision=HI)
        inner = jnp.einsum("iac,picb->piab", left_env[term_idx], mixed, precision=HI)
        partial_value = partial_value + jnp.einsum(
            "piac,ibc->piab", inner, right_env[term_idx], precision=HI
        )
    summed = lax.psum_scatter(partial_value, "term", scatter_dimension=2, tiled=True)
    return summed * row_mask


def per_device(start_vec, left_env, right_env, local_mpo, term_charge, sector_sizes, sector_ranks):
    width = start_vec.shape[3]
    row_count = start_vec.shape[2]
    states = start_vec.shape[0]
    sectors = start_vec.shape[1] * lax.axis_size("blk")
    row_start = lax.axis_index("term") * row_count
    row_ids = row_start + jnp.arange(row_count, dtype=jnp.int32)
    col_live = live_mask(sector_sizes, width)
    row_live = (row_ids[None, :] < sector_sizes[:, None]).astype(jnp.float32)
    row_mask = (row_live[:, :, None] * col_live[:, None, :])[None]
    start = start_vec * row_mask
    start_sq = lax.psum(jnp.sum(start * start), ("term", "blk"))
    vector = start / jnp.sqrt(start_sq + 1e-06)
    previous = jnp.zeros_like(vector)
    beta = jnp.float32(0.0)
    alphas = []
    betas = []
    for step in range(KRY):
        image = apply_operator(vector, left_env, right_env, local_mpo, term_charge, row_mask)
        alpha = lax.psum(jnp.sum(vector * image), ("term", "blk"))
        resid = image - alpha * vector - beta * previous
        norm_sq = lax.psum(jnp.sum(resid * resid), ("term", "blk"))
        new_beta = jnp.sqrt(norm_sq + 1e-06)
        previous = vector
        vector = resid / new_beta
        beta = new_beta
        alphas.append(alpha)
        betas.append(new_beta)
    coeffs = jnp.stack([jnp.stack(alphas), jnp.stack(betas)])
    krylov = jnp.sqrt(jnp.float32(sectors * states)) * width * vector
    whole = lax.all_gather(vector, "term", axis=2, tiled=True)
    gram = jnp.einsum("piab,picb->iac", vector, whole, precision=HI)
    kept_rows = (row_ids[None, :] < sector_ranks[:, None]).astype(jnp.float32)
    kept_cols = live_mask(sector_ranks, width)
    density = sectors * width * gram * kept_rows[:, :, None] * kept_cols[:, None, :]
    return (coeffs, krylov, density)


MESH = pl.DeviceIdType.MESH
BF = jnp.bfloat16
F32 = jnp.float32


def split(value):
    high = value.astype(BF)
    low = (value - high.astype(F32)).astype(BF)
    return high, low


def mm(left, right):
    return jnp.dot(left, right, preferred_element_type=F32)


def mm_t(left, right):
    return lax.dot_general(left, right, (((1,), (1,)), ((), ())), preferred_element_type=F32)


def lanczos_kernel(
    groups,
    start_ref, left_ref, right_ref, mpo_ref, charge_ref, sizes_ref, ranks_ref,
    coeffs_ref, krylov_ref, density_ref,
    meta_send_buf, counts_send, x_got, counts_got, l_got, r_got, meta_got,
    images, vectors, below, above, from_below, from_above,
    l_split, r_split, mixed, applied,
    pair_sums, all_sums, marks, coefs, out_send, den_send,
    init_send, init_recv, meta_send, meta_recv,
    halo_send, halo_recv, pair_send, pair_recv, all_send, all_recv,
    out_ssem, out_rsem,
):
    states, _, rows, width = start_ref.shape
    terms = left_ref.shape[0]
    t = lax.axis_index("term")
    b = lax.axis_index("blk")
    k = b // 2
    c = b % 2
    flip = k % 2
    me = t * 2 + c
    half = (t + flip) % 2
    part = (c + half) % 2
    sector = 4 * k + 2 * half + part
    has_lower = sector > 0
    has_upper = sector < 4 * groups - 1

    def owner(index):
        group = index // 4
        rest = index % 4
        own_half = rest // 2
        own_part = rest % 2
        return ((own_half + group) % 2, group * 2 + (own_part + own_half) % 2)

    lower_dev = owner(jnp.maximum(sector - 1, 0))
    upper_dev = owner(jnp.minimum(sector + 1, 4 * groups - 1))

    def pair_dev(step):
        other = (me + step) % 4
        return other, (other // 2, k * 2 + other % 2)

    def group_dev(step):
        other = (k + step) % groups
        return other, (t, other * 2 + c)

    for ref in (below, above, from_below, from_above, images, vectors):
        ref[...] = jnp.zeros_like(ref)

    barrier = pltpu.get_barrier_semaphore()
    for step in range(1, 4):
        pl.semaphore_signal(barrier, inc=1, device_id=pair_dev(step)[1], device_id_type=MESH)
    for step in range(1, groups):
        pl.semaphore_signal(barrier, inc=1, device_id=group_dev(step)[1], device_id_type=MESH)

    for w in range(terms):
        for p in range(states):
            for q in range(states):
                row = (w * states + p) * states + q
                meta_send_buf[row:row + 1, :] = jnp.full((1, width), mpo_ref[w, p, q], F32)
        row = terms * states * states + w
        meta_send_buf[row:row + 1, :] = jnp.full((1, width), charge_ref[w].astype(F32), F32)
    for s in range(2):
        counts_send[s, 0:1, :] = jnp.full((1, width), sizes_ref[s].astype(F32), F32)
        counts_send[s, 1:8, :] = jnp.full((7, width), ranks_ref[s].astype(F32), F32)

    pl.semaphore_wait(barrier, 3 + groups - 1)

    pieces = (
        (lambda s: start_ref.at[:, s], x_got),
        (lambda s: counts_send.at[s], counts_got),
        (lambda s: left_ref.at[:, s], l_got),
        (lambda s: right_ref.at[:, s], r_got),
    )
    target_t = (c + flip) % 2

    def init_copy(s, j):
        src, dst = pieces[j]
        return pltpu.make_async_remote_copy(
            src_ref=src(s), dst_ref=dst.at[t],
            send_sem=init_send.at[s, j], recv_sem=init_recv.at[t, j],
            device_id=(target_t, k * 2 + (s + c) % 2), device_id_type=MESH,
        )

    keeps = target_t == t
    partner = pair_dev(2)[1]
    meta_copy = pltpu.make_async_remote_copy(
        src_ref=meta_send_buf, dst_ref=meta_got.at[t],
        send_sem=meta_send, recv_sem=meta_recv,
        device_id=partner, device_id_type=MESH,
    )
    def own_copy(j):
        src, dst = pieces[j]
        return pltpu.make_async_copy(src(0), dst.at[t], init_recv.at[t, j])

    for j in range(4):
        @pl.when(jnp.logical_not(keeps))
        def _():
            init_copy(0, j).start()

        @pl.when(keeps)
        def _():
            own_copy(j).start()

        init_copy(1, j).start()
        if j == 1:
            meta_copy.start()

    meta_got[t] = meta_send_buf[...]

    def init_wait(source, j):
        src, dst = pieces[j]
        pltpu.make_async_remote_copy(
            src_ref=src(0), dst_ref=dst.at[source],
            send_sem=init_send.at[0, j], recv_sem=init_recv.at[source, j],
            device_id=partner, device_id_type=MESH,
        ).wait_recv()

    row_ids = lax.broadcasted_iota(jnp.int32, (width, width), 0).astype(F32)
    col_ids = lax.broadcasted_iota(jnp.int32, (width, width), 1).astype(F32)
    for source in range(2):
        init_wait(source, 0)
        init_wait(source, 1)
        size = counts_got[source, 0:1, :]
        at = source * rows
        live = (row_ids[at:at + rows] < size) & (col_ids[:rows] < size)
        for p in range(states):
            applied[p, pl.ds(at, rows), :] = jnp.where(live, x_got[source, p], 0.0)
    live_rows = row_ids < counts_got[0, 0:1, :]

    def lane_sums(first, second):
        total = first[0] * second[0]
        for p in range(1, states):
            total = total + first[p] * second[p]
        return jnp.sum(total, axis=0, keepdims=True)

    def write_products(slot, image, vector, before):
        pair_sums[slot, me] = jnp.concatenate(
            [
                lane_sums(image, image), lane_sums(vector, image), lane_sums(before, image),
                lane_sums(vector, vector), lane_sums(before, vector), lane_sums(before, before),
                jnp.zeros((2, width), F32),
            ],
            axis=0,
        )

    def pair_copy(slot, step):
        return pltpu.make_async_remote_copy(
            src_ref=pair_sums.at[slot, me], dst_ref=pair_sums.at[slot, me],
            send_sem=pair_send.at[step - 1], recv_sem=pair_recv.at[slot, me],
            device_id=pair_dev(step)[1], device_id_type=MESH,
        )

    def group_copy(slot, step):
        return pltpu.make_async_remote_copy(
            src_ref=all_sums.at[slot, k], dst_ref=all_sums.at[slot, k],
            send_sem=all_send.at[step - 1], recv_sem=all_recv.at[slot, k],
            device_id=group_dev(step)[1], device_id_type=MESH,
        )

    def start_pair(slot):
        for step in range(1, 4):
            pair_copy(slot, step).start()

    def finish_pair(slot):
        for step in range(1, 4):
            other, dev = pair_dev(step)
            pltpu.make_async_remote_copy(
                src_ref=pair_sums.at[slot, me], dst_ref=pair_sums.at[slot, other],
                send_sem=pair_send.at[step - 1], recv_sem=pair_recv.at[slot, other],
                device_id=dev, device_id_type=MESH,
            ).wait_recv()
        total = pair_sums[slot, 0]
        for other in range(1, 4):
            total = total + pair_sums[slot, other]
        all_sums[slot, k] = total
        for step in range(1, groups):
            group_copy(slot, step).start()

    def finish_sums(slot, beta_before):
        for step in range(1, groups):
            other, dev = group_dev(step)
            pltpu.make_async_remote_copy(
                src_ref=all_sums.at[slot, k], dst_ref=all_sums.at[slot, other],
                send_sem=all_send.at[step - 1], recv_sem=all_recv.at[slot, other],
                device_id=dev, device_id_type=MESH,
            ).wait_recv()
        total = all_sums[slot, 0]
        for other in range(1, groups):
            total = total + all_sums[slot, other]
        dots = jnp.broadcast_to(jnp.sum(total, axis=1, keepdims=True), total.shape)
        ww, vw, uw, vv, uv, uu = (dots[i:i + 1] for i in range(6))
        alpha = vw
        norm_sq = (
            ww - 2.0 * alpha * vw - 2.0 * beta_before * uw
            + alpha * alpha * vv + beta_before * beta_before * uu
            + 2.0 * alpha * beta_before * uv
        )
        beta = jnp.sqrt(jnp.maximum(norm_sq, 0.0) + 1e-06)
        for step in range(1, 4):
            pair_copy(slot, step).wait_send()
        for step in range(1, groups):
            group_copy(slot, step).wait_send()
        return alpha, beta

    chunk = states // 2

    def down_copy(slot, part_of):
        span = pl.ds(part_of * chunk, chunk)
        return pltpu.make_async_remote_copy(
            src_ref=applied.at[span], dst_ref=from_above.at[slot, span],
            send_sem=halo_send.at[0, part_of], recv_sem=halo_recv.at[slot, 0, part_of],
            device_id=lower_dev, device_id_type=MESH,
        )

    def up_copy(slot, part_of):
        span = pl.ds(part_of * chunk, chunk)
        return pltpu.make_async_remote_copy(
            src_ref=applied.at[span], dst_ref=from_below.at[slot, span],
            send_sem=halo_send.at[1, part_of], recv_sem=halo_recv.at[slot, 1, part_of],
            device_id=upper_dev, device_id_type=MESH,
        )

    def start_halo(slot, part_of):
        @pl.when(has_lower)
        def _():
            down_copy(slot, part_of).start()

        @pl.when(has_upper)
        def _():
            up_copy(slot, part_of).start()

    def wait_halo(slot, part_of):
        @pl.when(has_lower)
        def _():
            up_copy(slot, part_of).wait_recv()

        @pl.when(has_upper)
        def _():
            down_copy(slot, part_of).wait_recv()

    def wait_halo_send(slot, part_of):
        @pl.when(has_lower)
        def _():
            down_copy(slot, part_of).wait_send()

        @pl.when(has_upper)
        def _():
            up_copy(slot, part_of).wait_send()

    for part_of in range(2):
        start_halo(0, part_of)

    meta_copy.wait_recv()
    for source in range(2):
        init_wait(source, 2)
        for w in range(terms):
            high, low = split(jnp.where(live_rows, l_got[source, w], 0.0))
            l_split[source * terms + w] = jnp.concatenate([high, low], axis=1)
    for source in range(2):
        init_wait(source, 3)
        for w in range(terms):
            high, low = split(jnp.where(live_rows, r_got[source, w], 0.0).T)
            r_split[pl.ds((source * terms + w) * width, width), :] = jnp.concatenate([high, low], axis=1)

    def apply(slot, send):
        for w in range(2 * terms):
            source, local = w // terms, w % terms
            charge = meta_got[source, pl.ds(states * states * terms + local, 1), :]
            is_below = charge > 0.5
            is_above = charge < -0.5
            vec = jnp.concatenate(
                [
                    jnp.where(is_below, below[slot, q], jnp.where(is_above, above[slot, q], images[slot, q]))
                    for q in range(states)
                ],
                axis=1,
            )
            high, low = split(vec)
            both = l_split[w]
            inner = mm(both, jnp.concatenate([high, high], axis=0)) + mm(both[:, :width], low)
            for p in range(states):
                total = None
                for q in range(states):
                    row = local * states * states + p * states + q
                    factor = meta_got[source, pl.ds(row, 1), :]
                    piece = factor * inner[:, q * width:(q + 1) * width]
                    total = piece if total is None else total + piece
                high, low = split(total)
                mixed[pl.ds(p * width, width), pl.ds(w * width, width)] = high
                mixed[pl.ds((states + p) * width, width), pl.ds(w * width, width)] = low
        stacked = states * width
        span = chunk * width
        for part_of in range(2):
            top = mm(mixed[pl.ds(part_of * span, span), :], r_split[...])
            bottom = mm(mixed[pl.ds(stacked + part_of * span, span), :], r_split[:, :width])
            result = top[:, :width] + top[:, width:] + bottom
            for p in range(chunk):
                applied[part_of * chunk + p] = result[p * width:(p + 1) * width]

            @pl.when(send)
            def _():
                start_halo(1 - slot, part_of)

    lanes = lax.broadcasted_iota(jnp.int32, marks.shape, 1)
    subs = lax.broadcasted_iota(jnp.int32, marks.shape, 0)
    marks[...] = jnp.zeros_like(marks)

    def record(index, alpha, beta):
        here = lanes == index
        marks[...] = jnp.where(here & (subs == 0), alpha, jnp.where(here & (subs == 1), beta, marks[...]))

    def advance(slot, alpha, beta_before, scale):
        other = 1 - slot
        for p in range(states):
            image = images[other, p]
            vectors[slot, p] = (image - alpha * vectors[other, p] - beta_before * vectors[slot, p]) * scale
            images[slot, p] = (applied[p] - alpha * image - beta_before * images[slot, p]) * scale
        write_products(slot, images[slot], vectors[slot], vectors[other])
        start_pair(slot)

    def step_body(it, carry):
        alpha, beta_before, beta_next, scale = (coefs[i:i + 1, :] for i in range(4))
        slot = it % 2
        other = 1 - slot
        advance(slot, alpha, beta_before, scale)
        finish_pair(slot)
        for part_of in range(2):
            wait_halo(slot, part_of)
            for p in range(part_of * chunk, (part_of + 1) * chunk):
                for edge, got in ((below, from_below), (above, from_above)):
                    edge[slot, p] = (got[slot, p] - alpha * edge[other, p] - beta_before * edge[slot, p]) * scale
            wait_halo_send(slot, part_of)
        apply(slot, it < KRY - 1)
        alpha, beta = finish_sums(slot, beta_next)
        record(it - 1, alpha, beta)
        coefs[0:1, :] = alpha
        coefs[1:2, :] = beta_next
        coefs[2:3, :] = jnp.where(it == 0, 0.0, beta)
        coefs[3:4, :] = 1.0 / beta
        return carry

    coefs[0:3, :] = jnp.zeros((3, width), F32)
    coefs[3:4, :] = jnp.ones((1, width), F32)
    lax.fori_loop(0, KRY, step_body, 0)
    alpha, beta_before, beta_next, scale = (coefs[i:i + 1, :] for i in range(4))
    slot = KRY % 2
    advance(slot, alpha, beta_before, scale)
    finish_pair(slot)
    alpha, beta = finish_sums(slot, beta_next)
    beta_before = beta_next
    record(KRY - 1, alpha, beta)
    coeffs_ref[...] = marks[:2, :KRY]
    scale = 1.0 / beta
    last = [
        (images[slot, p] - alpha * vectors[slot, p] - beta_before * vectors[1 - slot, p]) * scale
        for p in range(states)
    ]
    sectors = 4 * groups
    stretch = float((sectors * states) ** 0.5) * width
    for p in range(states):
        for r in range(2):
            out_send[r, p] = stretch * last[p][r * rows:(r + 1) * rows]

    def krylov_copy(r):
        return pltpu.make_async_remote_copy(
            src_ref=out_send.at[r], dst_ref=krylov_ref.at[:, part],
            send_sem=out_ssem.at[0, r], recv_sem=out_rsem.at[0, part],
            device_id=(r, k * 2 + half), device_id_type=MESH,
        )

    def density_copy(r):
        return pltpu.make_async_remote_copy(
            src_ref=den_send.at[r], dst_ref=density_ref.at[part],
            send_sem=out_ssem.at[1, r], recv_sem=out_rsem.at[1, part],
            device_id=(r, k * 2 + half), device_id_type=MESH,
        )

    def is_self(r):
        return (t == r) & (half == c)

    for r in range(2):
        @pl.when(jnp.logical_not(is_self(r)))
        def _():
            krylov_copy(r).start()

        @pl.when(is_self(r))
        def _():
            pltpu.make_async_copy(out_send.at[r], krylov_ref.at[:, part], out_rsem.at[0, part]).start()

    high, low = split(jnp.concatenate(last, axis=1))
    gram = mm_t(high, high) + mm_t(high, low) + mm_t(low, high)
    rank = counts_got[0, 1:2, :]
    gram = jnp.where((row_ids < rank) & (col_ids < rank), float(sectors * width) * gram, 0.0)
    for r in range(2):
        den_send[r] = gram[r * rows:(r + 1) * rows]
    for r in range(2):
        @pl.when(jnp.logical_not(is_self(r)))
        def _():
            density_copy(r).start()

        @pl.when(is_self(r))
        def _():
            pltpu.make_async_copy(den_send.at[r], density_ref.at[part], out_rsem.at[1, part]).start()

    for s in range(2):
        for which, src, dst in ((0, out_send.at[0], krylov_ref.at[:, s]), (1, den_send.at[0], density_ref.at[s])):
            pltpu.make_async_remote_copy(
                src_ref=src, dst_ref=dst,
                send_sem=out_ssem.at[which, 0], recv_sem=out_rsem.at[which, s],
                device_id=partner, device_id_type=MESH,
            ).wait_recv()

    for r in range(2):
        @pl.when(jnp.logical_not(is_self(r)))
        def _():
            krylov_copy(r).wait_send()
            density_copy(r).wait_send()
    for j in range(4):
        @pl.when(jnp.logical_not(keeps))
        def _():
            init_copy(0, j).wait_send()
        init_copy(1, j).wait_send()
    meta_copy.wait_send()


def per_device_by_sector(start_vec, left_env, right_env, local_mpo, term_charge, sector_sizes, sector_ranks):
    states, _, rows, width = start_vec.shape
    terms = left_env.shape[0]
    groups = lax.axis_size("blk") // 2
    meta_rows = terms * states * states + terms
    meta_rows += -meta_rows % 8
    block = (states, width, width)
    dma = pltpu.SemaphoreType.DMA
    vmem = pl.BlockSpec(memory_space=pltpu.VMEM)
    smem = pl.BlockSpec(memory_space=pltpu.SMEM)
    hbm = pl.BlockSpec(memory_space=pltpu.HBM)

    def kernel(*refs):
        lanczos_kernel(groups, *refs)

    return pl.pallas_call(
        kernel,
        out_shape=(
            jax.ShapeDtypeStruct((2, KRY), F32),
            jax.ShapeDtypeStruct(start_vec.shape, F32),
            jax.ShapeDtypeStruct((2, rows, width), F32),
        ),
        in_specs=[hbm, hbm, hbm, smem, smem, smem, smem],
        out_specs=(vmem, hbm, hbm),
        scratch_shapes=[
            pltpu.VMEM((meta_rows, width), F32),
            pltpu.VMEM((2, 8, width), F32),
            pltpu.VMEM((2, states, rows, width), F32),
            pltpu.VMEM((2, 8, width), F32),
            pltpu.VMEM((2, terms, width, width), F32),
            pltpu.VMEM((2, terms, width, width), F32),
            pltpu.VMEM((2, meta_rows, width), F32),
            pltpu.VMEM((2,) + block, F32),
            pltpu.VMEM((2,) + block, F32),
            pltpu.VMEM((2,) + block, F32),
            pltpu.VMEM((2,) + block, F32),
            pltpu.VMEM((2,) + block, F32),
            pltpu.VMEM((2,) + block, F32),
            pltpu.VMEM((2 * terms, width, 2 * width), BF),
            pltpu.VMEM((2 * terms * width, 2 * width), BF),
            pltpu.VMEM((2 * states * width, 2 * terms * width), BF),
            pltpu.VMEM(block, F32),
            pltpu.VMEM((2, 4, 8, width), F32),
            pltpu.VMEM((2, groups, 8, width), F32),
            pltpu.VMEM((8, width), F32),
            pltpu.VMEM((8, width), F32),
            pltpu.VMEM((2, states, rows, width), F32),
            pltpu.VMEM((2, rows, width), F32),
            dma((2, 4)), dma((2, 4)), dma, dma,
            dma((2, 2)), dma((2, 2, 2)), dma((3,)), dma((2, 4)), dma((groups - 1,)), dma((2, groups)),
            dma((2, 2)), dma((2, 2)),
        ],
        compiler_params=pltpu.CompilerParams(
            collective_id=0, has_side_effects=True, vmem_limit_bytes=40 * 1024 * 1024
        ),
    )(start_vec, left_env, right_env, local_mpo, term_charge, sector_sizes, sector_ranks)


def solution(mesh):
    by_sector = mesh.shape["term"] == 2 and mesh.shape["blk"] % 2 == 0
    placed = (
        P(None, "blk", "term", None),
        P("term", "blk", None, None),
        P("term", "blk", None, None),
        P("term", None, None),
        P("term"),
        P("blk"),
        P("blk"),
    )
    return jax.shard_map(
        per_device_by_sector if by_sector else per_device,
        mesh=mesh,
        in_specs=placed,
        out_specs=(P(), P(None, "blk", "term", None), P("blk", "term", None)),
        check_vma=False,
    )
```

```python
import jax
import jax.numpy as jnp
from jax import lax
from jax.sharding import PartitionSpec as P
from jax.experimental import pallas as pl
from jax.experimental.pallas import tpu as pltpu

KRY = 8


HI = lax.Precision.HIGHEST


def from_behind(value, axis, by):
    devices = lax.axis_size(axis)
    pairs = [(i, i + by) for i in range(devices) if 0 <= i + by < devices]
    return lax.ppermute(value, axis, pairs)


def live_mask(counts, width):
    return (jnp.arange(width, dtype=jnp.int32)[None, :] < counts[:, None]).astype(jnp.float32)


def apply_operator(rows_vec, left_env, right_env, local_mpo, term_charge, row_mask):
    whole = lax.all_gather(rows_vec, "term", axis=2, tiled=True)
    lower_edge = from_behind(whole[:, -1:], "blk", 1)
    upper_edge = from_behind(whole[:, :1], "blk", -1)
    below = jnp.concatenate([lower_edge, whole[:, :-1]], axis=1)
    above = jnp.concatenate([whole[:, 1:], upper_edge], axis=1)
    partial_value = jnp.zeros_like(whole)
    for term_idx in range(left_env.shape[0]):
        charge = term_charge[term_idx]
        source = jnp.where(charge == 1, below, jnp.where(charge == -1, above, whole))
        mixed = jnp.einsum("pq,qiab->piab", local_mpo[term_idx], source, precision=HI)
        inner = jnp.einsum("iac,picb->piab", left_env[term_idx], mixed, precision=HI)
        partial_value = partial_value + jnp.einsum(
            "piac,ibc->piab", inner, right_env[term_idx], precision=HI
        )
    summed = lax.psum_scatter(partial_value, "term", scatter_dimension=2, tiled=True)
    return summed * row_mask


def per_device(start_vec, left_env, right_env, local_mpo, term_charge, sector_sizes, sector_ranks):
    width = start_vec.shape[3]
    row_count = start_vec.shape[2]
    states = start_vec.shape[0]
    sectors = start_vec.shape[1] * lax.axis_size("blk")
    row_start = lax.axis_index("term") * row_count
    row_ids = row_start + jnp.arange(row_count, dtype=jnp.int32)
    col_live = live_mask(sector_sizes, width)
    row_live = (row_ids[None, :] < sector_sizes[:, None]).astype(jnp.float32)
    row_mask = (row_live[:, :, None] * col_live[:, None, :])[None]
    start = start_vec * row_mask
    start_sq = lax.psum(jnp.sum(start * start), ("term", "blk"))
    vector = start / jnp.sqrt(start_sq + 1e-06)
    previous = jnp.zeros_like(vector)
    beta = jnp.float32(0.0)
    alphas = []
    betas = []
    for step in range(KRY):
        image = apply_operator(vector, left_env, right_env, local_mpo, term_charge, row_mask)
        alpha = lax.psum(jnp.sum(vector * image), ("term", "blk"))
        resid = image - alpha * vector - beta * previous
        norm_sq = lax.psum(jnp.sum(resid * resid), ("term", "blk"))
        new_beta = jnp.sqrt(norm_sq + 1e-06)
        previous = vector
        vector = resid / new_beta
        beta = new_beta
        alphas.append(alpha)
        betas.append(new_beta)
    coeffs = jnp.stack([jnp.stack(alphas), jnp.stack(betas)])
    krylov = jnp.sqrt(jnp.float32(sectors * states)) * width * vector
    whole = lax.all_gather(vector, "term", axis=2, tiled=True)
    gram = jnp.einsum("piab,picb->iac", vector, whole, precision=HI)
    kept_rows = (row_ids[None, :] < sector_ranks[:, None]).astype(jnp.float32)
    kept_cols = live_mask(sector_ranks, width)
    density = sectors * width * gram * kept_rows[:, :, None] * kept_cols[:, None, :]
    return (coeffs, krylov, density)


MESH = pl.DeviceIdType.MESH
BF = jnp.bfloat16
F32 = jnp.float32


def split(value):
    high = value.astype(BF)
    low = (value - high.astype(F32)).astype(BF)
    return high, low


def mm(left, right):
    return jnp.dot(left, right, preferred_element_type=F32)


def mm_t(left, right):
    return lax.dot_general(left, right, (((1,), (1,)), ((), ())), preferred_element_type=F32)


def lanczos_kernel(
    groups,
    start_ref, left_ref, right_ref, mpo_ref, charge_ref, sizes_ref, ranks_ref,
    coeffs_ref, krylov_ref, density_ref,
    meta_send_buf, counts_send, x_got, counts_got, l_got, r_got, meta_got,
    images, vectors, below, above, from_below, from_above,
    l_split, r_split, mixed, applied,
    pair_sums, all_sums, marks, coefs, out_send, den_send,
    init_send, init_recv, meta_send, meta_recv,
    halo_send, halo_recv, pair_send, pair_recv, all_send, all_recv,
    out_ssem, out_rsem,
):
    states, _, rows, width = start_ref.shape
    terms = left_ref.shape[0]
    t = lax.axis_index("term")
    b = lax.axis_index("blk")
    k = b // 2
    c = b % 2
    flip = k % 2
    me = t * 2 + c
    half = (t + flip) % 2
    part = (c + half) % 2
    sector = 4 * k + 2 * half + part
    has_lower = sector > 0
    has_upper = sector < 4 * groups - 1

    def owner(index):
        group = index // 4
        rest = index % 4
        own_half = rest // 2
        own_part = rest % 2
        return ((own_half + group) % 2, group * 2 + (own_part + own_half) % 2)

    lower_dev = owner(jnp.maximum(sector - 1, 0))
    upper_dev = owner(jnp.minimum(sector + 1, 4 * groups - 1))

    def pair_dev(step):
        other = (me + step) % 4
        return other, (other // 2, k * 2 + other % 2)

    def group_dev(step):
        other = (k + step) % groups
        return other, (t, other * 2 + c)

    for ref in (below, above, from_below, from_above, images, vectors):
        ref[...] = jnp.zeros_like(ref)

    barrier = pltpu.get_barrier_semaphore()
    for step in range(1, 4):
        pl.semaphore_signal(barrier, inc=1, device_id=pair_dev(step)[1], device_id_type=MESH)
    for step in range(1, groups):
        pl.semaphore_signal(barrier, inc=1, device_id=group_dev(step)[1], device_id_type=MESH)

    for w in range(terms):
        for p in range(states):
            for q in range(states):
                row = (w * states + p) * states + q
                meta_send_buf[row:row + 1, :] = jnp.full((1, width), mpo_ref[w, p, q], F32)
        row = terms * states * states + w
        meta_send_buf[row:row + 1, :] = jnp.full((1, width), charge_ref[w].astype(F32), F32)
    for s in range(2):
        counts_send[s, 0:1, :] = jnp.full((1, width), sizes_ref[s].astype(F32), F32)
        counts_send[s, 1:8, :] = jnp.full((7, width), ranks_ref[s].astype(F32), F32)

    pl.semaphore_wait(barrier, 3 + groups - 1)

    pieces = (
        (lambda s: start_ref.at[:, s], x_got),
        (lambda s: counts_send.at[s], counts_got),
        (lambda s: left_ref.at[:, s], l_got),
        (lambda s: right_ref.at[:, s], r_got),
    )
    target_t = (c + flip) % 2

    def init_copy(s, j):
        src, dst = pieces[j]
        return pltpu.make_async_remote_copy(
            src_ref=src(s), dst_ref=dst.at[t],
            send_sem=init_send.at[s, j], recv_sem=init_recv.at[t, j],
            device_id=(target_t, k * 2 + (s + c) % 2), device_id_type=MESH,
        )

    keeps = target_t == t
    partner = pair_dev(2)[1]
    meta_copy = pltpu.make_async_remote_copy(
        src_ref=meta_send_buf, dst_ref=meta_got.at[t],
        send_sem=meta_send, recv_sem=meta_recv,
        device_id=partner, device_id_type=MESH,
    )
    def own_copy(j):
        src, dst = pieces[j]
        return pltpu.make_async_copy(src(0), dst.at[t], init_recv.at[t, j])

    for j in range(4):
        @pl.when(jnp.logical_not(keeps))
        def _():
            init_copy(0, j).start()

        @pl.when(keeps)
        def _():
            own_copy(j).start()

        init_copy(1, j).start()
        if j == 1:
            meta_copy.start()

    meta_got[t] = meta_send_buf[...]

    def init_wait(source, j):
        src, dst = pieces[j]
        pltpu.make_async_remote_copy(
            src_ref=src(0), dst_ref=dst.at[source],
            send_sem=init_send.at[0, j], recv_sem=init_recv.at[source, j],
            device_id=partner, device_id_type=MESH,
        ).wait_recv()

    row_ids = lax.broadcasted_iota(jnp.int32, (width, width), 0).astype(F32)
    col_ids = lax.broadcasted_iota(jnp.int32, (width, width), 1).astype(F32)
    for source in range(2):
        init_wait(source, 0)
        init_wait(source, 1)
        size = counts_got[source, 0:1, :]
        at = source * rows
        live = (row_ids[at:at + rows] < size) & (col_ids[:rows] < size)
        for p in range(states):
            applied[p, pl.ds(at, rows), :] = jnp.where(live, x_got[source, p], 0.0)
    live_rows = row_ids < counts_got[0, 0:1, :]

    def lane_sums(first, second):
        total = first[0] * second[0]
        for p in range(1, states):
            total = total + first[p] * second[p]
        return jnp.sum(total, axis=0, keepdims=True)

    def write_products(slot, image, vector, before):
        pair_sums[slot, me] = jnp.concatenate(
            [
                lane_sums(image, image), lane_sums(vector, image), lane_sums(before, image),
                lane_sums(vector, vector), lane_sums(before, vector), lane_sums(before, before),
                jnp.zeros((2, width), F32),
            ],
            axis=0,
        )

    def pair_copy(slot, step):
        return pltpu.make_async_remote_copy(
            src_ref=pair_sums.at[slot, me], dst_ref=pair_sums.at[slot, me],
            send_sem=pair_send.at[step - 1], recv_sem=pair_recv.at[slot, me],
            device_id=pair_dev(step)[1], device_id_type=MESH,
        )

    def group_copy(slot, step):
        return pltpu.make_async_remote_copy(
            src_ref=all_sums.at[slot, k], dst_ref=all_sums.at[slot, k],
            send_sem=all_send.at[step - 1], recv_sem=all_recv.at[slot, k],
            device_id=group_dev(step)[1], device_id_type=MESH,
        )

    def start_pair(slot):
        for step in range(1, 4):
            pair_copy(slot, step).start()

    def finish_pair(slot):
        for step in range(1, 4):
            other, dev = pair_dev(step)
            pltpu.make_async_remote_copy(
                src_ref=pair_sums.at[slot, me], dst_ref=pair_sums.at[slot, other],
                send_sem=pair_send.at[step - 1], recv_sem=pair_recv.at[slot, other],
                device_id=dev, device_id_type=MESH,
            ).wait_recv()
        total = pair_sums[slot, 0]
        for other in range(1, 4):
            total = total + pair_sums[slot, other]
        all_sums[slot, k] = total
        for step in range(1, groups):
            group_copy(slot, step).start()

    def finish_sums(slot, beta_before):
        for step in range(1, groups):
            other, dev = group_dev(step)
            pltpu.make_async_remote_copy(
                src_ref=all_sums.at[slot, k], dst_ref=all_sums.at[slot, other],
                send_sem=all_send.at[step - 1], recv_sem=all_recv.at[slot, other],
                device_id=dev, device_id_type=MESH,
            ).wait_recv()
        total = all_sums[slot, 0]
        for other in range(1, groups):
            total = total + all_sums[slot, other]
        dots = jnp.broadcast_to(jnp.sum(total, axis=1, keepdims=True), total.shape)
        ww, vw, uw, vv, uv, uu = (dots[i:i + 1] for i in range(6))
        alpha = vw
        norm_sq = (
            ww - 2.0 * alpha * vw - 2.0 * beta_before * uw
            + alpha * alpha * vv + beta_before * beta_before * uu
            + 2.0 * alpha * beta_before * uv
        )
        beta = jnp.sqrt(jnp.maximum(norm_sq, 0.0) + 1e-06)
        for step in range(1, 4):
            pair_copy(slot, step).wait_send()
        for step in range(1, groups):
            group_copy(slot, step).wait_send()
        return alpha, beta

    chunk = states // 2

    def down_copy(slot, part_of):
        span = pl.ds(part_of * chunk, chunk)
        return pltpu.make_async_remote_copy(
            src_ref=applied.at[span], dst_ref=from_above.at[slot, span],
            send_sem=halo_send.at[0, part_of], recv_sem=halo_recv.at[slot, 0, part_of],
            device_id=lower_dev, device_id_type=MESH,
        )

    def up_copy(slot, part_of):
        span = pl.ds(part_of * chunk, chunk)
        return pltpu.make_async_remote_copy(
            src_ref=applied.at[span], dst_ref=from_below.at[slot, span],
            send_sem=halo_send.at[1, part_of], recv_sem=halo_recv.at[slot, 1, part_of],
            device_id=upper_dev, device_id_type=MESH,
        )

    def start_halo(slot, part_of):
        @pl.when(has_lower)
        def _():
            down_copy(slot, part_of).start()

        @pl.when(has_upper)
        def _():
            up_copy(slot, part_of).start()

    def wait_halo(slot, part_of):
        @pl.when(has_lower)
        def _():
            up_copy(slot, part_of).wait_recv()

        @pl.when(has_upper)
        def _():
            down_copy(slot, part_of).wait_recv()

    def wait_halo_send(slot, part_of):
        @pl.when(has_lower)
        def _():
            down_copy(slot, part_of).wait_send()

        @pl.when(has_upper)
        def _():
            up_copy(slot, part_of).wait_send()

    for part_of in range(2):
        start_halo(0, part_of)

    meta_copy.wait_recv()
    for source in range(2):
        init_wait(source, 2)
        for w in range(terms):
            high, low = split(jnp.where(live_rows, l_got[source, w], 0.0))
            l_split[source * terms + w] = jnp.concatenate([high, low], axis=1)
    for source in range(2):
        init_wait(source, 3)
        for w in range(terms):
            high, low = split(jnp.where(live_rows, r_got[source, w], 0.0).T)
            r_split[pl.ds((source * terms + w) * width, width), :] = jnp.concatenate([high, low], axis=1)

    def apply(slot, send):
        for w in range(2 * terms):
            source, local = w // terms, w % terms
            charge = meta_got[source, pl.ds(states * states * terms + local, 1), :]
            is_below = charge > 0.5
            is_above = charge < -0.5
            vec = jnp.concatenate(
                [
                    jnp.where(is_below, below[slot, q], jnp.where(is_above, above[slot, q], images[slot, q]))
                    for q in range(states)
                ],
                axis=1,
            )
            high, low = split(vec)
            both = l_split[w]
            inner = mm(both, jnp.concatenate([high, high], axis=0)) + mm(both[:, :width], low)
            for p in range(states):
                total = None
                for q in range(states):
                    row = local * states * states + p * states + q
                    factor = meta_got[source, pl.ds(row, 1), :]
                    piece = factor * inner[:, q * width:(q + 1) * width]
                    total = piece if total is None else total + piece
                high, low = split(total)
                mixed[pl.ds(p * width, width), pl.ds(w * width, width)] = high
                mixed[pl.ds((states + p) * width, width), pl.ds(w * width, width)] = low
        stacked = states * width
        span = chunk * width
        for part_of in range(2):
            top = mm(mixed[pl.ds(part_of * span, span), :], r_split[...])
            bottom = mm(mixed[pl.ds(stacked + part_of * span, span), :], r_split[:, :width])
            result = top[:, :width] + top[:, width:] + bottom
            for p in range(chunk):
                applied[part_of * chunk + p] = result[p * width:(p + 1) * width]

            @pl.when(send)
            def _():
                start_halo(1 - slot, part_of)

    lanes = lax.broadcasted_iota(jnp.int32, marks.shape, 1)
    subs = lax.broadcasted_iota(jnp.int32, marks.shape, 0)
    marks[...] = jnp.zeros_like(marks)

    def record(index, alpha, beta):
        here = lanes == index
        marks[...] = jnp.where(here & (subs == 0), alpha, jnp.where(here & (subs == 1), beta, marks[...]))

    def advance(slot, alpha, beta_before, scale):
        other = 1 - slot
        for p in range(states):
            image = images[other, p]
            vectors[slot, p] = (image - alpha * vectors[other, p] - beta_before * vectors[slot, p]) * scale
            images[slot, p] = (applied[p] - alpha * image - beta_before * images[slot, p]) * scale
        write_products(slot, images[slot], vectors[slot], vectors[other])
        start_pair(slot)

    def step_body(it, carry):
        alpha, beta_before, beta_next, scale = (coefs[i:i + 1, :] for i in range(4))
        slot = it % 2
        other = 1 - slot
        advance(slot, alpha, beta_before, scale)
        finish_pair(slot)
        for part_of in range(2):
            wait_halo(slot, part_of)
            for p in range(part_of * chunk, (part_of + 1) * chunk):
                for edge, got in ((below, from_below), (above, from_above)):
                    edge[slot, p] = (got[slot, p] - alpha * edge[other, p] - beta_before * edge[slot, p]) * scale
            wait_halo_send(slot, part_of)
        apply(slot, it < KRY - 1)
        alpha, beta = finish_sums(slot, beta_next)
        record(it - 1, alpha, beta)
        coefs[0:1, :] = alpha
        coefs[1:2, :] = beta_next
        coefs[2:3, :] = jnp.where(it == 0, 0.0, beta)
        coefs[3:4, :] = 1.0 / beta
        return carry

    coefs[0:3, :] = jnp.zeros((3, width), F32)
    coefs[3:4, :] = jnp.ones((1, width), F32)
    lax.fori_loop(0, KRY, step_body, 0)
    alpha, beta_before, beta_next, scale = (coefs[i:i + 1, :] for i in range(4))
    slot = KRY % 2
    advance(slot, alpha, beta_before, scale)
    finish_pair(slot)
    alpha, beta = finish_sums(slot, beta_next)
    beta_before = beta_next
    record(KRY - 1, alpha, beta)
    coeffs_ref[...] = marks[:2, :KRY]
    scale = 1.0 / beta
    last = [
        (images[slot, p] - alpha * vectors[slot, p] - beta_before * vectors[1 - slot, p]) * scale
        for p in range(states)
    ]
    sectors = 4 * groups
    stretch = float((sectors * states) ** 0.5) * width
    for p in range(states):
        for r in range(2):
            out_send[r, p] = stretch * last[p][r * rows:(r + 1) * rows]

    def krylov_copy(r):
        return pltpu.make_async_remote_copy(
            src_ref=out_send.at[r], dst_ref=krylov_ref.at[:, part],
            send_sem=out_ssem.at[0, r], recv_sem=out_rsem.at[0, part],
            device_id=(r, k * 2 + half), device_id_type=MESH,
        )

    def density_copy(r):
        return pltpu.make_async_remote_copy(
            src_ref=den_send.at[r], dst_ref=density_ref.at[part],
            send_sem=out_ssem.at[1, r], recv_sem=out_rsem.at[1, part],
            device_id=(r, k * 2 + half), device_id_type=MESH,
        )

    def is_self(r):
        return (t == r) & (half == c)

    for r in range(2):
        @pl.when(jnp.logical_not(is_self(r)))
        def _():
            krylov_copy(r).start()

        @pl.when(is_self(r))
        def _():
            pltpu.make_async_copy(out_send.at[r], krylov_ref.at[:, part], out_rsem.at[0, part]).start()

    high, low = split(jnp.concatenate(last, axis=1))
    gram = mm_t(high, high) + mm_t(high, low) + mm_t(low, high)
    rank = counts_got[0, 1:2, :]
    gram = jnp.where((row_ids < rank) & (col_ids < rank), float(sectors * width) * gram, 0.0)
    for r in range(2):
        den_send[r] = gram[r * rows:(r + 1) * rows]
    for r in range(2):
        @pl.when(jnp.logical_not(is_self(r)))
        def _():
            density_copy(r).start()

        @pl.when(is_self(r))
        def _():
            pltpu.make_async_copy(den_send.at[r], density_ref.at[part], out_rsem.at[1, part]).start()

    for s in range(2):
        for which, src, dst in ((0, out_send.at[0], krylov_ref.at[:, s]), (1, den_send.at[0], density_ref.at[s])):
            pltpu.make_async_remote_copy(
                src_ref=src, dst_ref=dst,
                send_sem=out_ssem.at[which, 0], recv_sem=out_rsem.at[which, s],
                device_id=partner, device_id_type=MESH,
            ).wait_recv()

    for r in range(2):
        @pl.when(jnp.logical_not(is_self(r)))
        def _():
            krylov_copy(r).wait_send()
            density_copy(r).wait_send()
    for j in range(4):
        @pl.when(jnp.logical_not(keeps))
        def _():
            init_copy(0, j).wait_send()
        init_copy(1, j).wait_send()
    meta_copy.wait_send()


def per_device_by_sector(start_vec, left_env, right_env, local_mpo, term_charge, sector_sizes, sector_ranks):
    states, _, rows, width = start_vec.shape
    terms = left_env.shape[0]
    groups = lax.axis_size("blk") // 2
    meta_rows = terms * states * states + terms
    meta_rows += -meta_rows % 8
    block = (states, width, width)
    dma = pltpu.SemaphoreType.DMA
    vmem = pl.BlockSpec(memory_space=pltpu.VMEM)
    smem = pl.BlockSpec(memory_space=pltpu.SMEM)
    hbm = pl.BlockSpec(memory_space=pltpu.HBM)

    def kernel(*refs):
        lanczos_kernel(groups, *refs)

    return pl.pallas_call(
        kernel,
        out_shape=(
            jax.ShapeDtypeStruct((2, KRY), F32),
            jax.ShapeDtypeStruct(start_vec.shape, F32),
            jax.ShapeDtypeStruct((2, rows, width), F32),
        ),
        in_specs=[hbm, hbm, hbm, smem, smem, smem, smem],
        out_specs=(vmem, hbm, hbm),
        scratch_shapes=[
            pltpu.VMEM((meta_rows, width), F32),
            pltpu.VMEM((2, 8, width), F32),
            pltpu.VMEM((2, states, rows, width), F32),
            pltpu.VMEM((2, 8, width), F32),
            pltpu.VMEM((2, terms, width, width), F32),
            pltpu.VMEM((2, terms, width, width), F32),
            pltpu.VMEM((2, meta_rows, width), F32),
            pltpu.VMEM((2,) + block, F32),
            pltpu.VMEM((2,) + block, F32),
            pltpu.VMEM((2,) + block, F32),
            pltpu.VMEM((2,) + block, F32),
            pltpu.VMEM((2,) + block, F32),
            pltpu.VMEM((2,) + block, F32),
            pltpu.VMEM((2 * terms, width, 2 * width), BF),
            pltpu.VMEM((2 * terms * width, 2 * width), BF),
            pltpu.VMEM((2 * states * width, 2 * terms * width), BF),
            pltpu.VMEM(block, F32),
            pltpu.VMEM((2, 4, 8, width), F32),
            pltpu.VMEM((2, groups, 8, width), F32),
            pltpu.VMEM((8, width), F32),
            pltpu.VMEM((8, width), F32),
            pltpu.VMEM((2, states, rows, width), F32),
            pltpu.VMEM((2, rows, width), F32),
            dma((2, 4)), dma((2, 4)), dma, dma,
            dma((2, 2)), dma((2, 2, 2)), dma((3,)), dma((2, 4)), dma((groups - 1,)), dma((2, groups)),
            dma((2, 2)), dma((2, 2)),
        ],
        compiler_params=pltpu.CompilerParams(
            collective_id=0, has_side_effects=True, vmem_limit_bytes=63 * 1024 * 1024
        ),
    )(start_vec, left_env, right_env, local_mpo, term_charge, sector_sizes, sector_ranks)


def solution(mesh):
    by_sector = mesh.shape["term"] == 2 and mesh.shape["blk"] % 2 == 0
    placed = (
        P(None, "blk", "term", None),
        P("term", "blk", None, None),
        P("term", "blk", None, None),
        P("term", None, None),
        P("term"),
        P("blk"),
        P("blk"),
    )
    return jax.shard_map(
        per_device_by_sector if by_sector else per_device,
        mesh=mesh,
        in_specs=placed,
        out_specs=(P(), P(None, "blk", "term", None), P("blk", "term", None)),
        check_vma=False,
    )
```
